32 devices in a mesh: row: 4 (over x, core), col: 8 (over z, y).
Axes of the slice: x: 2, y: 2, z: 4, core: 2. Of those that a mesh axis runs over, the one named last changes fastest.
Arguments:
- stiffness: bfloat16 [896, 256, 256], P(('row', 'col')), may hold values from -0.25 to 0.25
- stiffness_index: int32 [896, 2], P(('row', 'col')), may hold values from 0 to 15
- mode_basis: bfloat16 [131072, 256], P(('row', 'col')), may hold values from -0.75 to 0.75
- pair_owner: int32 [32, 2], replicated, may hold values from 0 to 1
- margin: int32 [32, 2, 4, 2], replicated, may hold values from 0 to 15
Outputs:
- coarse: bfloat16 [32, 32, 256, 256], P('row', None, 'col')
The draws below stay inside these ranges and needn't reach their ends.
All inputs are finite; a program needn't handle non-finite values.
Results may differ from the reference program's by a relative error of at most 0.0049.
Values may be sent and summed in bfloat16 or wider, within the bound.
A program may use at most 128 MiB of HBM per device.

```python
import jax
import jax.numpy as jnp
import numpy as np
from jax import lax

M = 256
BS = 256
NB = 16
NK = 28
OVB = 4
NLOC = 4096
S = 32
N_ROW = 4
N_COL = 8


def with_ends(array, own_key, smallest, top_value):
    spot = [jax.random.randint(jax.random.fold_in(own_key, axis), (), 0, length) for axis, length in enumerate(array.shape)]
    longest = array.shape.index(max(array.shape))
    beside = spot[:longest] + [(spot[longest] + 1) % array.shape[longest]] + spot[longest + 1:]
    return array.at[tuple(spot)].set(smallest).at[tuple(beside)].set(top_value)


def block_scale(rng, dims, split, low, high):
    gain = 1.0
    for dim, blocks in split:
        steps = jax.random.uniform(jax.random.fold_in(jax.random.fold_in(rng, 6), dim), (blocks,), jnp.float32, low / len(split), high / len(split))
        gain = gain * jnp.repeat(jnp.exp(steps), dims[dim] // blocks).reshape((-1,) + (1,) * (len(dims) - 1 - dim))
    return gain


def centred(stream_key, dims, deviation, reach, shards=(), kind=jnp.bfloat16):
    values = deviation * jax.random.normal(stream_key, dims, jnp.float32)
    if shards:
        values = values * block_scale(stream_key, dims, shards, -0.22, 0.18)
    return jnp.clip(values, -reach, reach).astype(kind)


def setup_inputs(seed: int = 0) -> dict:
    keys = jax.random.split(jax.random.key(seed), 6)
    return {
        "stiffness": centred(keys[0], (S * NK, BS, BS), (2 * BS) ** -0.5, 0.25, ((0, 32),)),
        "stiffness_index": with_ends(jax.random.randint(keys[1], (S * NK, 2), 0, NB), jax.random.fold_in(keys[1], 1), 0, NB - 1).astype(jnp.int32),
        "mode_basis": centred(keys[2], (S * NLOC, M), 0.125, 0.75, ((0, 32),)),
        "pair_owner": with_ends(jax.random.randint(keys[3], (S, 2), 0, 2), jax.random.fold_in(keys[3], 1), 0, 1).astype(jnp.int32),
        "margin": with_ends(jax.random.randint(keys[4], (S, 2, OVB, 2), 0, NB), jax.random.fold_in(keys[4], 1), 0, NB - 1).astype(jnp.int32),
    }


def reference(stiffness, stiffness_index, mode_basis, pair_owner, margin):
    blocks_all = stiffness.reshape(S, NK, BS, BS)
    index_all = stiffness_index.reshape(S, NK, 2)
    modes_all = mode_basis.reshape(S, NB, BS, M)

    def local_apply(inputs):
        stiff_blocks, indices, mode_blocks = inputs
        picked = mode_blocks[indices[:, 1]]
        products = jnp.einsum('kab,kbm->kam', stiff_blocks.astype(jnp.float32), picked.astype(jnp.float32),
                              precision=lax.Precision.HIGHEST)
        selector = (indices[:, 0][None, :] == jnp.arange(NB, dtype=jnp.int32)[:, None]).astype(jnp.float32)
        summed = jnp.einsum('nk,kam->nam', selector, products, precision=lax.Precision.HIGHEST)
        applied = summed.astype(jnp.bfloat16)
        diagonal = jnp.dot(mode_blocks.reshape(NLOC, M).T, applied.reshape(NLOC, M),
                           preferred_element_type=jnp.float32).astype(jnp.bfloat16)
        return applied, diagonal

    applied_all, diagonals = lax.map(local_apply, (blocks_all, index_all, modes_all))

    def project_pair(inputs):
        first, second, direction = inputs
        owner_flag = pair_owner[first, direction]
        lists = margin[first, direction]
        own_modes = modes_all[first][lists[:, 0]]
        own_applied = applied_all[first][lists[:, 0]]
        far_modes = modes_all[second][lists[:, 1]]
        far_applied = applied_all[second][lists[:, 1]]
        left = jnp.where(owner_flag == 0, own_modes, own_applied).reshape(OVB * BS, M)
        right = jnp.where(owner_flag == 0, far_applied, far_modes).reshape(OVB * BS, M)
        return jnp.dot(left.T, right, preferred_element_type=jnp.float32).astype(jnp.bfloat16)

    numbers = np.arange(S, dtype=np.int32)
    group_of = numbers // N_COL
    place_of = numbers % N_COL
    col_first = numbers[place_of < N_COL - 1]
    row_first = numbers[group_of < N_ROW - 1]
    firsts = np.concatenate([col_first, row_first]).astype(np.int32)
    seconds = np.concatenate([col_first + 1, row_first + N_COL]).astype(np.int32)
    directions = np.concatenate([np.zeros(col_first.shape[0], np.int32), np.ones(row_first.shape[0], np.int32)])
    pair_blocks = lax.map(project_pair, (jnp.asarray(firsts), jnp.asarray(seconds), jnp.asarray(directions)))

    result = jnp.zeros((S, S, M, M), jnp.bfloat16)
    result = result.at[numbers, numbers].set(diagonals)
    result = result.at[firsts, seconds].set(pair_blocks)
    return result
```

```python
import functools

import jax
import jax.numpy as jnp
from jax import lax
from jax.experimental import pallas as pl
from jax.experimental.pallas import tpu as pltpu
from jax.sharding import PartitionSpec as P

MESH = pl.DeviceIdType.MESH
F32 = jnp.float32
BF16 = jnp.bfloat16


def tdot(left, right):
    return lax.dot_general(left, right, (((0,), (0,)), ((), ())), preferred_element_type=F32)


def exchange_kernel(
    n_row, n_col, group,
    table, index, owner, margin, stiff_hbm, modes_hbm, out,
    stiff, modes, sums, applied, far_out, far_in, slots, held, total,
    stiff_sem, modes_sem, far_send, far_recv, piece_send, piece_recv,
):
    block_total, size, width = stiff.shape
    blocks = modes.shape[0]
    shared = far_out.shape[1]
    my_row = lax.axis_index("row")
    my_col = lax.axis_index("col")
    here = my_row * n_col + my_col
    has_next = (my_col < n_col - 1, my_row < n_row - 1)
    has_prev = (my_col > 0, my_row > 0)
    prev_id = ({"col": jnp.maximum(my_col - 1, 0)}, {"row": jnp.maximum(my_row - 1, 0)})
    next_row = {"row": jnp.minimum(my_row + 1, n_row - 1)}

    modes_copy = pltpu.make_async_copy(modes_hbm, modes, modes_sem)
    modes_copy.start()

    def stiff_copy(c):
        part = pl.ds(c * group, group)
        return pltpu.make_async_copy(stiff_hbm.at[part], stiff.at[part], stiff_sem.at[c])

    def start_stiff(c, carry):
        stiff_copy(c).start()
        return carry

    lax.fori_loop(0, block_total // group, start_stiff, 0)

    barrier = pltpu.get_barrier_semaphore()
    for d in range(1, n_col):
        pl.semaphore_signal(
            barrier, inc=1, device_id={"col": lax.rem(my_col + d, n_col)}, device_id_type=MESH
        )

    @pl.when(has_prev[1])
    def _():
        pl.semaphore_signal(barrier, inc=1, device_id=prev_id[1], device_id_type=MESH)

    @pl.when(has_next[1])
    def _():
        pl.semaphore_signal(barrier, inc=1, device_id=next_row, device_id_type=MESH)

    sums[0] = jnp.zeros((size, width), F32)
    modes_copy.wait()

    def apply_group(c, carry):
        stiff_copy(c).wait()
        for q in range(group):
            k = c * group + q
            product = jnp.dot(stiff[k], modes[index[1, k]], preferred_element_type=F32)
            sums[k + 1] = sums[table[k]] + product
        return carry

    lax.fori_loop(0, block_total // group, apply_group, 0)

    sides = has_prev[1].astype(jnp.int32) + has_next[1].astype(jnp.int32)
    pl.semaphore_wait(barrier, n_col - 1 + sides)

    def far_copy(d, i):
        return pltpu.make_async_remote_copy(
            src_ref=far_out.at[d, i], dst_ref=far_in.at[d, i],
            send_sem=far_send.at[d, i], recv_sem=far_recv.at[d, i],
            device_id=prev_id[d], device_id_type=MESH,
        )

    for d in range(2):
        @pl.when(has_prev[d])
        def _():
            first = here - (1 if d == 0 else n_col)
            flag = owner[d, first]
            for i in range(shared):
                pick = margin[d, i, 1, first]
                far_out[d, i] = jnp.where(
                    flag == 0, sums[table[block_total + pick]].astype(BF16), modes[pick]
                )
                far_copy(d, i).start()

    def piece_copy(slot, d):
        return pltpu.make_async_remote_copy(
            src_ref=slots.at[slot, lax.rem(my_col + d, n_col)], dst_ref=held.at[slot, my_col],
            send_sem=piece_send.at[slot, d], recv_sem=piece_recv.at[slot, d],
            device_id={"col": lax.rem(my_col + d, n_col)}, device_id_type=MESH,
        )

    def scatter(slot, value):
        slots[slot] = value.astype(BF16).reshape(slots.shape[1:])
        for d in range(1, n_col):
            piece_copy(slot, d).start()
        held[slot, my_col] = slots[slot, my_col]

    def round_block(a, carry):
        applied[a] = sums[table[block_total + a]].astype(BF16)
        return carry

    lax.fori_loop(0, blocks, round_block, 0)
    step = 4 if blocks % 4 == 0 else 1
    total[...] = jnp.zeros_like(total)

    def diagonal_step(c, carry):
        part = pl.ds(c * step, step)
        total[...] += tdot(
            modes[part].reshape(step * size, width), applied[part].reshape(step * size, width)
        )
        return carry

    lax.fori_loop(0, blocks // step, diagonal_step, 0)
    scatter(0, total[...])

    for d in (1, 0):
        @pl.when(has_next[d])
        def _():
            flag = owner[d, here]
            value = None
            for i in range(shared):
                pick = margin[d, i, 0, here]
                near = jnp.where(flag == 0, modes[pick], applied[pick])
                far_copy(d, i).wait_recv()
                term = tdot(near, far_in[d, i])
                value = term if value is None else value + term
            scatter(d + 1, value)

    @pl.when(jnp.logical_not(has_next[1]))
    def _():
        held[2] = jnp.zeros(held.shape[1:], BF16)

    held[1, n_col - 1] = jnp.zeros(held.shape[2:], BF16)

    for d in range(2):
        @pl.when(has_prev[d])
        def _():
            for i in range(shared):
                far_copy(d, i).wait_send()

    def wait_piece(slot, d):
        source = lax.rem(my_col + n_col - d, n_col)
        return pltpu.make_async_remote_copy(
            src_ref=slots.at[slot, my_col], dst_ref=held.at[slot, source],
            send_sem=piece_send.at[slot, d], recv_sem=piece_recv.at[slot, d],
            device_id={"col": lax.rem(my_col + d, n_col)}, device_id_type=MESH,
        )

    for d in range(1, n_col):
        wait_piece(0, d).wait_recv()
        piece_copy(0, d).wait_send()

    @pl.when(has_next[1])
    def _():
        for d in range(1, n_col):
            wait_piece(2, d).wait_recv()
            piece_copy(2, d).wait_send()

    for d in range(1, n_col):
        @pl.when(lax.rem(my_col + n_col - d, n_col) < n_col - 1)
        def _():
            wait_piece(1, d).wait_recv()

        @pl.when(has_next[0])
        def _():
            piece_copy(1, d).wait_send()

    out[...] = held[...]


def place_kernel(n_row, n_col, held, out):
    i = pl.program_id(0)
    my_row = lax.axis_index("row")
    out[...] = jnp.zeros_like(out)
    spot = my_row * n_col + i
    out[0, spot] = held[0, i]

    @pl.when(i < n_col - 1)
    def _():
        out[0, spot + 1] = held[1, i]

    @pl.when(my_row < n_row - 1)
    def _():
        out[0, spot + n_col] = held[2, i]


def on_device(stiffness, stiffness_index, mode_basis, pair_owner, margin):
    n_row = lax.axis_size("row")
    n_col = lax.axis_size("col")
    count, size, _ = stiffness.shape
    width = mode_basis.shape[1]
    blocks = mode_basis.shape[0] // size
    shared = margin.shape[2]
    rows = width // n_col
    group = 4 if count % 4 == 0 else 1
    mine = stiffness_index[:, 0]
    number = jnp.arange(count, dtype=jnp.int32)
    wanted = jnp.concatenate([mine, jnp.arange(blocks, dtype=jnp.int32)])
    limit = jnp.concatenate([number, jnp.full((blocks,), count, jnp.int32)])
    match = (wanted[:, None] == mine[None, :]) & (number[None, :] < limit[:, None])
    table = jnp.max(jnp.where(match, number[None, :] + 1, 0), axis=1)

    smem = pl.BlockSpec(memory_space=pltpu.SMEM)
    hbm = pl.BlockSpec(memory_space=pl.ANY)
    held = pl.pallas_call(
        functools.partial(exchange_kernel, n_row, n_col, group),
        out_shape=jax.ShapeDtypeStruct((3, n_col, rows, width), BF16),
        in_specs=[smem] * 4 + [hbm] * 2,
        out_specs=pl.BlockSpec(memory_space=pltpu.VMEM),
        scratch_shapes=[
            pltpu.VMEM((count, size, size), BF16),
            pltpu.VMEM((blocks, size, width), BF16),
            pltpu.VMEM((count + 1, size, width), F32),
            pltpu.VMEM((blocks, size, width), BF16),
            pltpu.VMEM((2, shared, size, width), BF16),
            pltpu.VMEM((2, shared, size, width), BF16),
            pltpu.VMEM((3, n_col, rows, width), BF16),
            pltpu.VMEM((3, n_col, rows, width), BF16),
            pltpu.VMEM((width, width), F32),
            pltpu.SemaphoreType.DMA((count // group,)),
            pltpu.SemaphoreType.DMA,
            pltpu.SemaphoreType.DMA((2, shared)),
            pltpu.SemaphoreType.DMA((2, shared)),
            pltpu.SemaphoreType.DMA((3, n_col)),
            pltpu.SemaphoreType.DMA((3, n_col)),
        ],
        compiler_params=pltpu.CompilerParams(
            collective_id=0, has_side_effects=True, vmem_limit_bytes=56 * 1024 * 1024
        ),
        name="exchange",
    )(
        table,
        stiffness_index.T,
        pair_owner.T,
        margin.transpose(1, 2, 3, 0),
        stiffness,
        mode_basis.reshape(blocks, size, width),
    )
    places = n_row * n_col
    return pl.pallas_call(
        functools.partial(place_kernel, n_row, n_col),
        out_shape=jax.ShapeDtypeStruct((n_col, places, rows, width), BF16),
        grid=(n_col,),
        in_specs=[pl.BlockSpec((3, n_col, rows, width), lambda i: (0, 0, 0, 0))],
        out_specs=pl.BlockSpec((1, places, rows, width), lambda i: (i, 0, 0, 0)),
        compiler_params=pltpu.CompilerParams(vmem_limit_bytes=40 * 1024 * 1024),
        name="place",
    )(held)


def solution(mesh):
    return jax.shard_map(
        on_device,
        mesh=mesh,
        in_specs=(
            P(("row", "col"), None, None),
            P(("row", "col"), None),
            P(("row", "col"), None),
            P(),
            P(),
        ),
        out_specs=P("row", None, "col", None),
        check_vma=False,
    )
```

```python
import functools

import jax
import jax.numpy as jnp
from jax import lax
from jax.experimental import pallas as pl
from jax.experimental.pallas import tpu as pltpu
from jax.sharding import PartitionSpec as P

MESH = pl.DeviceIdType.MESH
F32 = jnp.float32
BF16 = jnp.bfloat16


def tdot(left, right):
    return lax.dot_general(left, right, (((0,), (0,)), ((), ())), preferred_element_type=F32)


def exchange_kernel(
    n_row, n_col, group,
    index, owner, margin, stiff_hbm, modes_hbm, out,
    stiff, modes, products, sums, applied, far_out, far_in, slots, held, total, before, last,
    stiff_sem, modes_sem, far_send, far_recv, piece_send, piece_recv,
):
    block_total, size, width = stiff.shape
    blocks = modes.shape[0]
    shared = far_out.shape[1]
    my_row = lax.axis_index("row")
    my_col = lax.axis_index("col")
    here = my_row * n_col + my_col
    back = lax.rem(my_row, 2)
    ends = (my_col - 1 + 2 * back, my_row - 1)
    starts = (my_col + 1 - 2 * back, my_row + 1)
    sends = (jnp.logical_and(ends[0] >= 0, ends[0] < n_col), ends[1] >= 0)
    takes = (jnp.logical_and(starts[0] >= 0, starts[0] < n_col), starts[1] < n_row)
    send_first = (here - 1 + back, here - n_col)
    take_first = (here - back, here)
    send_side = (1 - back, 1)
    take_side = (back, 0)
    target = ({"col": jnp.clip(ends[0], 0, n_col - 1)}, {"row": jnp.maximum(ends[1], 0)})
    next_row = {"row": jnp.minimum(starts[1], n_row - 1)}

    modes_copy = pltpu.make_async_copy(modes_hbm, modes, modes_sem)
    modes_copy.start()

    def stiff_copy(c):
        part = pl.ds(c * group, group)
        return pltpu.make_async_copy(stiff_hbm.at[part], stiff.at[part], stiff_sem.at[c])

    def start_stiff(c, carry):
        stiff_copy(c).start()
        return carry

    lax.fori_loop(0, block_total // group, start_stiff, 0)

    barrier = pltpu.get_barrier_semaphore()
    for d in range(1, n_col):
        pl.semaphore_signal(
            barrier, inc=1, device_id={"col": lax.rem(my_col + d, n_col)}, device_id_type=MESH
        )

    @pl.when(sends[1])
    def _():
        pl.semaphore_signal(barrier, inc=1, device_id=target[1], device_id_type=MESH)

    @pl.when(takes[1])
    def _():
        pl.semaphore_signal(barrier, inc=1, device_id=next_row, device_id_type=MESH)

    sums[0] = jnp.zeros((size, width), F32)
    latest = [jnp.int32(0)] * blocks
    for k in range(block_total):
        mine = index[0, k]
        found = jnp.int32(0)
        for a in range(blocks):
            hit = mine == a
            found = jnp.where(hit, latest[a], found)
            latest[a] = jnp.where(hit, k + 1, latest[a])
        before[k] = found
    for a in range(blocks):
        last[a] = latest[a]
    modes_copy.wait()

    def apply_group(c, carry):
        stiff_copy(c).wait()
        for q in range(group):
            k = c * group + q
            products[q] = jnp.dot(stiff[k], modes[index[1, k]], preferred_element_type=F32)
        for q in range(group):
            k = c * group + q
            sums[k + 1] = sums[before[k]] + products[q]
        return carry

    lax.fori_loop(0, block_total // group, apply_group, 0)

    sides = sends[1].astype(jnp.int32) + takes[1].astype(jnp.int32)
    pl.semaphore_wait(barrier, n_col - 1 + sides)

    def far_copy(d, i):
        return pltpu.make_async_remote_copy(
            src_ref=far_out.at[d, i], dst_ref=far_in.at[d, i],
            send_sem=far_send.at[d, i], recv_sem=far_recv.at[d, i],
            device_id=target[d], device_id_type=MESH,
        )

    for d in range(2):
        @pl.when(sends[d])
        def _():
            first = send_first[d]
            flag = owner[d, first]
            for i in range(shared):
                pick = margin[d, i, send_side[d], first]
                far_out[d, i] = jnp.where(
                    flag + send_side[d] == 1, sums[last[pick]].astype(BF16), modes[pick]
                )
                far_copy(d, i).start()

    def piece_copy(slot, d):
        place = my_col - back if slot == 1 else my_col
        peer = lax.rem(my_col + d, n_col)
        return pltpu.make_async_remote_copy(
            src_ref=slots.at[slot, peer], dst_ref=held.at[slot, place],
            send_sem=piece_send.at[slot, d], recv_sem=piece_recv.at[slot, d],
            device_id={"col": peer}, device_id_type=MESH,
        )

    def scatter(slot, value):
        place = my_col - back if slot == 1 else my_col
        slots[slot] = value.astype(BF16).reshape(slots.shape[1:])
        for d in range(1, n_col):
            piece_copy(slot, d).start()
        held[slot, place] = slots[slot, my_col]

    def round_block(a, carry):
        applied[a] = sums[last[a]].astype(BF16)
        return carry

    lax.fori_loop(0, blocks, round_block, 0)
    step = 4 if blocks % 4 == 0 else 1
    total[...] = jnp.zeros_like(total)

    def diagonal_step(c, carry):
        part = pl.ds(c * step, step)
        total[...] += tdot(
            modes[part].reshape(step * size, width), applied[part].reshape(step * size, width)
        )
        return carry

    lax.fori_loop(0, blocks // step, diagonal_step, 0)
    scatter(0, total[...])

    for d in (1, 0):
        @pl.when(takes[d])
        def _():
            first = take_first[d]
            flag = owner[d, first]
            value = None
            for i in range(shared):
                pick = margin[d, i, take_side[d], first]
                near = jnp.where(flag + take_side[d] == 1, applied[pick], modes[pick])
                far_copy(d, i).wait_recv()
                far = far_in[d, i]
                if d == 0:
                    near, far = jnp.where(back == 0, near, far), jnp.where(back == 0, far, near)
                term = tdot(near, far)
                value = term if value is None else value + term
            scatter(d + 1, value)

    @pl.when(jnp.logical_not(takes[1]))
    def _():
        held[2] = jnp.zeros(held.shape[1:], BF16)

    held[1, n_col - 1] = jnp.zeros(held.shape[2:], BF16)

    for d in range(2):
        @pl.when(sends[d])
        def _():
            for i in range(shared):
                far_copy(d, i).wait_send()

    def wait_piece(slot, d):
        source = lax.rem(my_col + n_col - d, n_col)
        place = jnp.clip(source - back, 0, n_col - 1) if slot == 1 else source
        return pltpu.make_async_remote_copy(
            src_ref=slots.at[slot, my_col], dst_ref=held.at[slot, place],
            send_sem=piece_send.at[slot, d], recv_sem=piece_recv.at[slot, d],
            device_id={"col": lax.rem(my_col + d, n_col)}, device_id_type=MESH,
        )

    for d in range(1, n_col):
        wait_piece(0, d).wait_recv()
        piece_copy(0, d).wait_send()

    @pl.when(takes[1])
    def _():
        for d in range(1, n_col):
            wait_piece(2, d).wait_recv()
            piece_copy(2, d).wait_send()

    for d in range(1, n_col):
        origin = lax.rem(my_col + n_col - d, n_col) + 1 - 2 * back

        @pl.when(jnp.logical_and(origin >= 0, origin < n_col))
        def _():
            wait_piece(1, d).wait_recv()

        @pl.when(takes[0])
        def _():
            piece_copy(1, d).wait_send()

    out[...] = held[...]


def place_kernel(n_row, n_col, held_hbm, out, held, zeros, same, after, held_sem, out_sem):
    my_row = lax.axis_index("row")
    fetch = pltpu.make_async_copy(held_hbm, held, held_sem)
    fetch.start()
    zeros[...] = jnp.zeros_like(zeros)

    def write(source, g):
        return pltpu.make_async_copy(source, out.at[:, g], out_sem.at[g])

    for g in range(n_row):
        @pl.when(jnp.logical_and(g != my_row, g != my_row + 1))
        def _():
            write(zeros, g).start()

    same[...] = jnp.zeros_like(same)
    after[...] = jnp.zeros_like(after)
    fetch.wait()
    for i in range(n_col):
        same[i, i] = held[0, i]
        if i < n_col - 1:
            same[i, i + 1] = held[1, i]
    write(same, my_row).start()

    @pl.when(my_row < n_row - 1)
    def _():
        for i in range(n_col):
            after[i, i] = held[2, i]
        write(after, my_row + 1).start()

    for g in range(n_row):
        write(zeros, g).wait()


def on_device(stiffness, stiffness_index, mode_basis, pair_owner, margin):
    n_row = lax.axis_size("row")
    n_col = lax.axis_size("col")
    count, size, _ = stiffness.shape
    width = mode_basis.shape[1]
    blocks = mode_basis.shape[0] // size
    shared = margin.shape[2]
    rows = width // n_col
    group = max(q for q in range(1, 9) if count % q == 0)
    smem = pl.BlockSpec(memory_space=pltpu.SMEM)
    hbm = pl.BlockSpec(memory_space=pl.ANY)
    held = pl.pallas_call(
        functools.partial(exchange_kernel, n_row, n_col, group),
        out_shape=jax.ShapeDtypeStruct((3, n_col, rows, width), BF16),
        in_specs=[smem] * 3 + [hbm] * 2,
        out_specs=pl.BlockSpec(memory_space=pltpu.VMEM),
        scratch_shapes=[
            pltpu.VMEM((count, size, size), BF16),
            pltpu.VMEM((blocks, size, width), BF16),
            pltpu.VMEM((group, size, width), F32),
            pltpu.VMEM((count + 1, size, width), F32),
            pltpu.VMEM((blocks, size, width), BF16),
            pltpu.VMEM((2, shared, size, width), BF16),
            pltpu.VMEM((2, shared, size, width), BF16),
            pltpu.VMEM((3, n_col, rows, width), BF16),
            pltpu.VMEM((3, n_col, rows, width), BF16),
            pltpu.VMEM((width, width), F32),
            pltpu.SMEM((count,), jnp.int32),
            pltpu.SMEM((blocks,), jnp.int32),
            pltpu.SemaphoreType.DMA((count // group,)),
            pltpu.SemaphoreType.DMA,
            pltpu.SemaphoreType.DMA((2, shared)),
            pltpu.SemaphoreType.DMA((2, shared)),
            pltpu.SemaphoreType.DMA((3, n_col)),
            pltpu.SemaphoreType.DMA((3, n_col)),
        ],
        compiler_params=pltpu.CompilerParams(
            collective_id=0, has_side_effects=True, vmem_limit_bytes=56 * 1024 * 1024
        ),
        name="exchange",
    )(
        stiffness_index.T,
        pair_owner.T,
        margin.transpose(1, 2, 3, 0),
        stiffness,
        mode_basis.reshape(blocks, size, width),
    )
    part = (n_col, n_col, rows, width)
    coarse = pl.pallas_call(
        functools.partial(place_kernel, n_row, n_col),
        out_shape=jax.ShapeDtypeStruct((n_col, n_row, n_col, rows, width), BF16),
        in_specs=[hbm],
        out_specs=hbm,
        scratch_shapes=[
            pltpu.VMEM((3, n_col, rows, width), BF16),
            pltpu.VMEM(part, BF16),
            pltpu.VMEM(part, BF16),
            pltpu.VMEM(part, BF16),
            pltpu.SemaphoreType.DMA,
            pltpu.SemaphoreType.DMA((n_row,)),
        ],
        compiler_params=pltpu.CompilerParams(vmem_limit_bytes=56 * 1024 * 1024),
        name="place",
    )(held)
    return coarse.reshape(n_col, n_row * n_col, rows, width)


def solution(mesh):
    return jax.shard_map(
        on_device,
        mesh=mesh,
        in_specs=(
            P(("row", "col"), None, None),
            P(("row", "col"), None),
            P(("row", "col"), None),
            P(),
            P(),
        ),
        out_specs=P("row", None, "col", None),
        check_vma=False,
    )
```

```python
import functools

import jax
import jax.numpy as jnp
from jax import lax
from jax.experimental import pallas as pl
from jax.experimental.pallas import tpu as pltpu
from jax.sharding import PartitionSpec as P

MESH = pl.DeviceIdType.MESH
F32 = jnp.float32
BF16 = jnp.bfloat16


def tdot(left, right):
    return lax.dot_general(left, right, (((0,), (0,)), ((), ())), preferred_element_type=F32)


def exchange_kernel(
    n_row, n_col, group, passes,
    index, owner, margin, stiff_hbm, modes_hbm, out,
    stiff, modes, products, sums, applied, far_out, far_in, slots, held, total, before, last,
    stiff_sem, modes_sem, far_send, far_recv, piece_send, piece_recv,
):
    block_total, size, width = stiff.shape
    blocks = modes.shape[0]
    shared = far_out.shape[1] // passes
    half = size // passes
    my_row = lax.axis_index("row")
    my_col = lax.axis_index("col")
    here = my_row * n_col + my_col
    back = lax.rem(my_row, 2)
    ends = (my_col - 1 + 2 * back, my_row - 1)
    starts = (my_col + 1 - 2 * back, my_row + 1)
    sends = (jnp.logical_and(ends[0] >= 0, ends[0] < n_col), ends[1] >= 0)
    takes = (jnp.logical_and(starts[0] >= 0, starts[0] < n_col), starts[1] < n_row)
    send_first = (here - 1 + back, here - n_col)
    take_first = (here - back, here)
    send_side = (1 - back, 1)
    take_side = (back, 0)
    target = ({"col": jnp.clip(ends[0], 0, n_col - 1)}, {"row": jnp.maximum(ends[1], 0)})
    next_row = {"row": jnp.minimum(starts[1], n_row - 1)}

    modes_copy = pltpu.make_async_copy(modes_hbm, modes, modes_sem)
    modes_copy.start()

    chunks = block_total // group

    def stiff_copy(h, c):
        part = (pl.ds(c * group, group), pl.ds(h * half, half))
        return pltpu.make_async_copy(stiff_hbm.at[part], stiff.at[part], stiff_sem.at[h, c])

    for h in range(passes):
        for c in range(chunks):
            stiff_copy(h, c).start()

    barrier = pltpu.get_barrier_semaphore()
    for d in range(1, n_col):
        pl.semaphore_signal(
            barrier, inc=1, device_id={"col": lax.rem(my_col + d, n_col)}, device_id_type=MESH
        )

    @pl.when(sends[1])
    def _():
        pl.semaphore_signal(barrier, inc=1, device_id=target[1], device_id_type=MESH)

    @pl.when(takes[1])
    def _():
        pl.semaphore_signal(barrier, inc=1, device_id=next_row, device_id_type=MESH)

    sums[0] = jnp.zeros((size, width), F32)
    latest = [jnp.int32(0)] * blocks
    for k in range(block_total):
        mine = index[0, k]
        found = jnp.int32(0)
        for a in range(blocks):
            hit = mine == a
            found = jnp.where(hit, latest[a], found)
            latest[a] = jnp.where(hit, k + 1, latest[a])
        before[k] = found
    for a in range(blocks):
        last[a] = latest[a]
    modes_copy.wait()

    def far_copy(d, j):
        return pltpu.make_async_remote_copy(
            src_ref=far_out.at[d, j], dst_ref=far_in.at[d, j],
            send_sem=far_send.at[d, j], recv_sem=far_recv.at[d, j],
            device_id=target[d], device_id_type=MESH,
        )

    sides = sends[1].astype(jnp.int32) + takes[1].astype(jnp.int32)
    for h in range(passes):
        rows = pl.ds(h * half, half)

        def apply_group(c, carry):
            stiff_copy(h, c).wait()
            for q in range(group):
                k = c * group + q
                products[q] = jnp.dot(
                    stiff[k, rows], modes[index[1, k]], preferred_element_type=F32
                )
            for q in range(group):
                k = c * group + q
                sums[k + 1, rows] = sums[before[k], rows] + products[q]
            return carry

        lax.fori_loop(0, chunks, apply_group, 0)
        if h == 0:
            pl.semaphore_wait(barrier, n_col - 1 + sides)
        for d in range(2):
            @pl.when(sends[d])
            def _():
                first = send_first[d]
                flag = owner[d, first]
                for i in range(shared):
                    pick = margin[d, i, send_side[d], first]
                    j = h * shared + i
                    far_out[d, j] = jnp.where(
                        flag + send_side[d] == 1,
                        sums[last[pick], rows].astype(BF16),
                        modes[pick, rows],
                    )
                    far_copy(d, j).start()

    def piece_copy(slot, d):
        place = my_col - back if slot == 1 else my_col
        peer = lax.rem(my_col + d, n_col)
        return pltpu.make_async_remote_copy(
            src_ref=slots.at[slot, peer], dst_ref=held.at[slot, place],
            send_sem=piece_send.at[slot, d], recv_sem=piece_recv.at[slot, d],
            device_id={"col": peer}, device_id_type=MESH,
        )

    def scatter(slot, value):
        place = my_col - back if slot == 1 else my_col
        slots[slot] = value.astype(BF16).reshape(slots.shape[1:])
        for d in range(1, n_col):
            piece_copy(slot, d).start()
        held[slot, place] = slots[slot, my_col]

    def round_block(a, carry):
        applied[a] = sums[last[a]].astype(BF16)
        return carry

    lax.fori_loop(0, blocks, round_block, 0)
    step = 4 if blocks % 4 == 0 else 1
    total[...] = jnp.zeros_like(total)

    def diagonal_step(c, carry):
        part = pl.ds(c * step, step)
        total[...] += tdot(
            modes[part].reshape(step * size, width), applied[part].reshape(step * size, width)
        )
        return carry

    lax.fori_loop(0, blocks // step, diagonal_step, 0)
    scatter(0, total[...])

    for d in (1, 0):
        @pl.when(takes[d])
        def _():
            first = take_first[d]
            flag = owner[d, first]
            value = None
            for j in range(passes * shared):
                h, i = divmod(j, shared)
                rows = pl.ds(h * half, half)
                pick = margin[d, i, take_side[d], first]
                near = jnp.where(
                    flag + take_side[d] == 1, applied[pick, rows], modes[pick, rows]
                )
                far_copy(d, j).wait_recv()
                far = far_in[d, j]
                if d == 0:
                    near, far = jnp.where(back == 0, near, far), jnp.where(back == 0, far, near)
                term = tdot(near, far)
                value = term if value is None else value + term
            scatter(d + 1, value)

    @pl.when(jnp.logical_not(takes[1]))
    def _():
        held[2] = jnp.zeros(held.shape[1:], BF16)

    held[1, n_col - 1] = jnp.zeros(held.shape[2:], BF16)

    for d in range(2):
        @pl.when(sends[d])
        def _():
            for j in range(passes * shared):
                far_copy(d, j).wait_send()

    def wait_piece(slot, d):
        source = lax.rem(my_col + n_col - d, n_col)
        place = jnp.clip(source - back, 0, n_col - 1) if slot == 1 else source
        return pltpu.make_async_remote_copy(
            src_ref=slots.at[slot, my_col], dst_ref=held.at[slot, place],
            send_sem=piece_send.at[slot, d], recv_sem=piece_recv.at[slot, d],
            device_id={"col": lax.rem(my_col + d, n_col)}, device_id_type=MESH,
        )

    for d in range(1, n_col):
        wait_piece(0, d).wait_recv()
        piece_copy(0, d).wait_send()

    @pl.when(takes[1])
    def _():
        for d in range(1, n_col):
            wait_piece(2, d).wait_recv()
            piece_copy(2, d).wait_send()

    for d in range(1, n_col):
        origin = lax.rem(my_col + n_col - d, n_col) + 1 - 2 * back

        @pl.when(jnp.logical_and(origin >= 0, origin < n_col))
        def _():
            wait_piece(1, d).wait_recv()

        @pl.when(takes[0])
        def _():
            piece_copy(1, d).wait_send()

    out[...] = held[...]


def place_kernel(n_row, n_col, held, out, zeros, same, after, out_sem):
    my_row = lax.axis_index("row")
    zeros[...] = jnp.zeros_like(zeros)

    def write(source, g):
        return pltpu.make_async_copy(source, out.at[:, g], out_sem.at[g])

    for g in range(n_row):
        @pl.when(jnp.logical_and(g != my_row, g != my_row + 1))
        def _():
            write(zeros, g).start()

    same[...] = jnp.zeros_like(same)
    after[...] = jnp.zeros_like(after)
    for i in range(n_col):
        same[i, i] = held[0, i]
        if i < n_col - 1:
            same[i, i + 1] = held[1, i]
    write(same, my_row).start()

    @pl.when(my_row < n_row - 1)
    def _():
        for i in range(n_col):
            after[i, i] = held[2, i]
        write(after, my_row + 1).start()

    for g in range(n_row):
        write(zeros, g).wait()


def on_device(stiffness, stiffness_index, mode_basis, pair_owner, margin):
    n_row = lax.axis_size("row")
    n_col = lax.axis_size("col")
    count, size, _ = stiffness.shape
    width = mode_basis.shape[1]
    blocks = mode_basis.shape[0] // size
    shared = margin.shape[2]
    rows = width // n_col
    group = max(q for q in range(1, 9) if count % q == 0)
    smem = pl.BlockSpec(memory_space=pltpu.SMEM)
    hbm = pl.BlockSpec(memory_space=pltpu.HBM)
    vmem = pl.BlockSpec(memory_space=pltpu.VMEM)
    passes = 2
    held = pl.pallas_call(
        functools.partial(exchange_kernel, n_row, n_col, group, passes),
        out_shape=jax.ShapeDtypeStruct((3, n_col, rows, width), BF16),
        in_specs=[smem] * 3 + [hbm] * 2,
        out_specs=pl.BlockSpec(memory_space=pltpu.VMEM),
        scratch_shapes=[
            pltpu.VMEM((count, size, size), BF16),
            pltpu.VMEM((blocks, size, width), BF16),
            pltpu.VMEM((group, size // passes, width), F32),
            pltpu.VMEM((count + 1, size, width), F32),
            pltpu.VMEM((blocks, size, width), BF16),
            pltpu.VMEM((2, passes * shared, size // passes, width), BF16),
            pltpu.VMEM((2, passes * shared, size // passes, width), BF16),
            pltpu.VMEM((3, n_col, rows, width), BF16),
            pltpu.VMEM((3, n_col, rows, width), BF16),
            pltpu.VMEM((width, width), F32),
            pltpu.SMEM((count,), jnp.int32),
            pltpu.SMEM((blocks,), jnp.int32),
            pltpu.SemaphoreType.DMA((passes, count // group)),
            pltpu.SemaphoreType.DMA,
            pltpu.SemaphoreType.DMA((2, passes * shared)),
            pltpu.SemaphoreType.DMA((2, passes * shared)),
            pltpu.SemaphoreType.DMA((3, n_col)),
            pltpu.SemaphoreType.DMA((3, n_col)),
        ],
        compiler_params=pltpu.CompilerParams(
            collective_id=0, has_side_effects=True, vmem_limit_bytes=53 * 1024 * 1024
        ),
        name="exchange",
    )(
        stiffness_index.T,
        pair_owner.T,
        margin.transpose(1, 2, 3, 0),
        stiffness,
        mode_basis.reshape(blocks, size, width),
    )
    part = (n_col, n_col, rows, width)
    coarse = pl.pallas_call(
        functools.partial(place_kernel, n_row, n_col),
        out_shape=jax.ShapeDtypeStruct((n_col, n_row, n_col, rows, width), BF16),
        in_specs=[vmem],
        out_specs=hbm,
        scratch_shapes=[
            pltpu.VMEM(part, BF16),
            pltpu.VMEM(part, BF16),
            pltpu.VMEM(part, BF16),
            pltpu.SemaphoreType.DMA((n_row,)),
        ],
        compiler_params=pltpu.CompilerParams(vmem_limit_bytes=53 * 1024 * 1024),
        name="place",
    )(held)
    return coarse.reshape(n_col, n_row * n_col, rows, width)


def solution(mesh):
    return jax.shard_map(
        on_device,
        mesh=mesh,
        in_specs=(
            P(("row", "col"), None, None),
            P(("row", "col"), None),
            P(("row", "col"), None),
            P(),
            P(),
        ),
        out_specs=P("row", None, "col", None),
        check_vma=False,
    )
```

```python
import functools

import jax
import jax.numpy as jnp
from jax import lax
from jax.experimental import pallas as pl
from jax.experimental.pallas import tpu as pltpu
from jax.sharding import PartitionSpec as P

MESH = pl.DeviceIdType.MESH
F32 = jnp.float32
BF16 = jnp.bfloat16


def tdot(left, right):
    return lax.dot_general(left, right, (((0,), (0,)), ((), ())), preferred_element_type=F32)


def exchange_kernel(
    n_row, n_col, group, passes,
    index, owner, margin, stiff_hbm, modes_hbm, out,
    stiff, modes, products, sums, applied, far_out, far_in, slots, held, total, before, last,
    stiff_sem, modes_sem, far_send, far_recv, piece_send, piece_recv,
):
    block_total, size, width = stiff.shape
    blocks = modes.shape[0]
    shared = far_out.shape[1] // passes
    half = width // passes
    my_row = lax.axis_index("row")
    my_col = lax.axis_index("col")
    here = my_row * n_col + my_col
    back = lax.rem(my_row, 2)
    ends = (my_col - 1 + 2 * back, my_row - 1)
    starts = (my_col + 1 - 2 * back, my_row + 1)
    sends = (jnp.logical_and(ends[0] >= 0, ends[0] < n_col), ends[1] >= 0)
    takes = (jnp.logical_and(starts[0] >= 0, starts[0] < n_col), starts[1] < n_row)
    send_first = (here - 1 + back, here - n_col)
    take_first = (here - back, here)
    send_side = (1 - back, 1)
    take_side = (back, 0)
    target = ({"col": jnp.clip(ends[0], 0, n_col - 1)}, {"row": jnp.maximum(ends[1], 0)})
    next_row = {"row": jnp.minimum(starts[1], n_row - 1)}

    modes_copy = pltpu.make_async_copy(modes_hbm, modes, modes_sem)
    modes_copy.start()

    chunks = block_total // group

    def stiff_copy(c):
        part = pl.ds(c * group, group)
        return pltpu.make_async_copy(stiff_hbm.at[part], stiff.at[part], stiff_sem.at[c])

    for c in range(chunks):
        stiff_copy(c).start()

    barrier = pltpu.get_barrier_semaphore()
    for d in range(1, n_col):
        pl.semaphore_signal(
            barrier, inc=1, device_id={"col": lax.rem(my_col + d, n_col)}, device_id_type=MESH
        )

    @pl.when(sends[1])
    def _():
        pl.semaphore_signal(barrier, inc=1, device_id=target[1], device_id_type=MESH)

    @pl.when(takes[1])
    def _():
        pl.semaphore_signal(barrier, inc=1, device_id=next_row, device_id_type=MESH)

    sums[0] = jnp.zeros((size, width), F32)
    latest = [jnp.int32(0)] * blocks
    for k in range(block_total):
        mine = index[0, k]
        found = jnp.int32(0)
        for a in range(blocks):
            hit = mine == a
            found = jnp.where(hit, latest[a], found)
            latest[a] = jnp.where(hit, k + 1, latest[a])
        before[k] = found
    for a in range(blocks):
        last[a] = latest[a]
    modes_copy.wait()

    def far_copy(d, j):
        return pltpu.make_async_remote_copy(
            src_ref=far_out.at[d, j], dst_ref=far_in.at[d, j],
            send_sem=far_send.at[d, j], recv_sem=far_recv.at[d, j],
            device_id=target[d], device_id_type=MESH,
        )

    sides = sends[1].astype(jnp.int32) + takes[1].astype(jnp.int32)
    for h in range(passes):
        cols = pl.ds(h * half, half)

        def apply_group(c, carry):
            if h == 0:
                stiff_copy(c).wait()
            for q in range(group):
                k = c * group + q
                products[q] = jnp.dot(
                    stiff[k], modes[index[1, k], :, cols], preferred_element_type=F32
                )
            for q in range(group):
                k = c * group + q
                sums[k + 1, :, cols] = sums[before[k], :, cols] + products[q]
            return carry

        lax.fori_loop(0, chunks, apply_group, 0)
        if h == 0:
            pl.semaphore_wait(barrier, n_col - 1 + sides)
        for d in range(2):
            @pl.when(sends[d])
            def _():
                first = send_first[d]
                flag = owner[d, first]
                for i in range(shared):
                    pick = margin[d, i, send_side[d], first]
                    j = h * shared + i
                    far_out[d, j] = jnp.where(
                        flag + send_side[d] == 1,
                        sums[last[pick], :, cols].astype(BF16),
                        modes[pick, :, cols],
                    )
                    far_copy(d, j).start()

    def piece_copy(slot, d, place):
        peer = lax.rem(my_col + d, n_col)
        return pltpu.make_async_remote_copy(
            src_ref=slots.at[slot, peer], dst_ref=held.at[slot, place],
            send_sem=piece_send.at[slot, d], recv_sem=piece_recv.at[slot, d],
            device_id={"col": peer}, device_id_type=MESH,
        )

    def part_copy(h, d, place):
        peer = lax.rem(my_col + d, n_col)
        cols = pl.ds(h * half, half)
        return pltpu.make_async_remote_copy(
            src_ref=slots.at[1, peer, :, cols], dst_ref=held.at[1, place, :, cols],
            send_sem=piece_send.at[1 + 2 * h, d], recv_sem=piece_recv.at[1 + 2 * h, d],
            device_id={"col": peer}, device_id_type=MESH,
        )

    def scatter(slot):
        for d in range(1, n_col):
            piece_copy(slot, d, my_col).start()
        held[slot, my_col] = slots[slot, my_col]

    def round_block(a, carry):
        applied[a] = sums[last[a]].astype(BF16)
        return carry

    lax.fori_loop(0, blocks, round_block, 0)
    step = 4 if blocks % 4 == 0 else 1
    total[...] = jnp.zeros_like(total)

    def diagonal_step(c, carry):
        part = pl.ds(c * step, step)
        total[...] += tdot(
            modes[part].reshape(step * size, width), applied[part].reshape(step * size, width)
        )
        return carry

    lax.fori_loop(0, blocks // step, diagonal_step, 0)
    slots[0] = total[...].astype(BF16).reshape(slots.shape[1:])
    scatter(0)

    def pair_part(d, h, near_left):
        first = take_first[d]
        flag = owner[d, first]
        value = None
        for i in range(shared):
            pick = margin[d, i, take_side[d], first]
            near = jnp.where(flag + take_side[d] == 1, applied[pick], modes[pick])
            far = far_in[d, h * shared + i]
            term = tdot(near, far) if near_left else tdot(far, near)
            value = term if value is None else value + term
        return value.astype(BF16)

    def wait_far(d, h):
        for i in range(shared):
            far_copy(d, h * shared + i).wait_recv()

    @pl.when(takes[1])
    def _():
        for h in range(passes):
            wait_far(1, h)
            slots[2, :, :, pl.ds(h * half, half)] = pair_part(1, h, True).reshape(
                n_col, slots.shape[2], half
            )
        scatter(2)

    per = n_col // passes
    for h in range(passes):
        @pl.when(jnp.logical_and(takes[0], back == 0))
        def _():
            wait_far(0, h)
            cols = pl.ds(h * half, half)
            slots[1, :, :, cols] = pair_part(0, h, True).reshape(n_col, slots.shape[2], half)
            for d in range(1, n_col):
                part_copy(h, d, my_col).start()
            held[1, my_col, :, cols] = slots[1, my_col, :, cols]

        @pl.when(jnp.logical_and(takes[0], back == 1))
        def _():
            wait_far(0, h)
            slots[1, pl.ds(h * per, per)] = pair_part(0, h, False).reshape(
                per, slots.shape[2], width
            )
            for d in range(1, n_col):
                @pl.when(lax.rem(my_col + d, n_col) // per == h)
                def _():
                    piece_copy(1, d, my_col - 1).start()

            @pl.when(my_col // per == h)
            def _():
                held[1, my_col - 1] = slots[1, my_col]

    @pl.when(jnp.logical_not(takes[1]))
    def _():
        held[2] = jnp.zeros(held.shape[1:], BF16)

    held[1, n_col - 1] = jnp.zeros(held.shape[2:], BF16)

    for d in range(2):
        @pl.when(sends[d])
        def _():
            for j in range(passes * shared):
                far_copy(d, j).wait_send()

    for d in range(1, n_col):
        source = lax.rem(my_col + n_col - d, n_col)
        piece_copy(0, d, source).wait_recv()
        piece_copy(0, d, my_col).wait_send()

    @pl.when(takes[1])
    def _():
        for d in range(1, n_col):
            source = lax.rem(my_col + n_col - d, n_col)
            piece_copy(2, d, source).wait_recv()
            piece_copy(2, d, my_col).wait_send()

    for d in range(1, n_col):
        source = lax.rem(my_col + n_col - d, n_col)

        @pl.when(jnp.logical_and(back == 0, source < n_col - 1))
        def _():
            for h in range(passes):
                part_copy(h, d, source).wait_recv()

        @pl.when(jnp.logical_and(back == 1, source > 0))
        def _():
            piece_copy(1, d, source - 1).wait_recv()

        @pl.when(jnp.logical_and(takes[0], back == 0))
        def _():
            for h in range(passes):
                part_copy(h, d, my_col).wait_send()

        @pl.when(jnp.logical_and(takes[0], back == 1))
        def _():
            piece_copy(1, d, my_col - 1).wait_send()

    out[...] = held[...]


def place_kernel(n_row, n_col, held_hbm, out, held, zeros, same, after, held_sem, out_sem):
    my_row = lax.axis_index("row")
    fetch = pltpu.make_async_copy(held_hbm, held, held_sem)
    fetch.start()
    zeros[...] = jnp.zeros_like(zeros)

    def write(source, g):
        return pltpu.make_async_copy(source, out.at[:, g], out_sem.at[g])

    for g in range(n_row):
        @pl.when(jnp.logical_and(g != my_row, g != my_row + 1))
        def _():
            write(zeros, g).start()

    same[...] = jnp.zeros_like(same)
    after[...] = jnp.zeros_like(after)
    fetch.wait()
    for i in range(n_col):
        same[i, i] = held[0, i]
        if i < n_col - 1:
            same[i, i + 1] = held[1, i]
    write(same, my_row).start()

    @pl.when(my_row < n_row - 1)
    def _():
        for i in range(n_col):
            after[i, i] = held[2, i]
        write(after, my_row + 1).start()

    for g in range(n_row):
        write(zeros, g).wait()


def on_device(stiffness, stiffness_index, mode_basis, pair_owner, margin):
    n_row = lax.axis_size("row")
    n_col = lax.axis_size("col")
    count, size, _ = stiffness.shape
    width = mode_basis.shape[1]
    blocks = mode_basis.shape[0] // size
    shared = margin.shape[2]
    rows = width // n_col
    group = max(q for q in range(1, 9) if count % q == 0)
    smem = pl.BlockSpec(memory_space=pltpu.SMEM)
    hbm = pl.BlockSpec(memory_space=pl.ANY)
    passes = 2
    held = pl.pallas_call(
        functools.partial(exchange_kernel, n_row, n_col, group, passes),
        out_shape=jax.ShapeDtypeStruct((3, n_col, rows, width), BF16),
        in_specs=[smem] * 3 + [hbm] * 2,
        out_specs=pl.BlockSpec(memory_space=pltpu.VMEM),
        scratch_shapes=[
            pltpu.VMEM((count, size, size), BF16),
            pltpu.VMEM((blocks, size, width), BF16),
            pltpu.VMEM((group, size, width // passes), F32),
            pltpu.VMEM((count + 1, size, width), F32),
            pltpu.VMEM((blocks, size, width), BF16),
            pltpu.VMEM((2, passes * shared, size, width // passes), BF16),
            pltpu.VMEM((2, passes * shared, size, width // passes), BF16),
            pltpu.VMEM((3, n_col, rows, width), BF16),
            pltpu.VMEM((3, n_col, rows, width), BF16),
            pltpu.VMEM((width, width), F32),
            pltpu.SMEM((count,), jnp.int32),
            pltpu.SMEM((blocks,), jnp.int32),
            pltpu.SemaphoreType.DMA((count // group,)),
            pltpu.SemaphoreType.DMA,
            pltpu.SemaphoreType.DMA((2, passes * shared)),
            pltpu.SemaphoreType.DMA((2, passes * shared)),
            pltpu.SemaphoreType.DMA((4, n_col)),
            pltpu.SemaphoreType.DMA((4, n_col)),
        ],
        compiler_params=pltpu.CompilerParams(
            collective_id=0, has_side_effects=True, vmem_limit_bytes=56 * 1024 * 1024
        ),
        name="exchange",
    )(
        stiffness_index.T,
        pair_owner.T,
        margin.transpose(1, 2, 3, 0),
        stiffness,
        mode_basis.reshape(blocks, size, width),
    )
    part = (n_col, n_col, rows, width)
    coarse = pl.pallas_call(
        functools.partial(place_kernel, n_row, n_col),
        out_shape=jax.ShapeDtypeStruct((n_col, n_row, n_col, rows, width), BF16),
        in_specs=[hbm],
        out_specs=hbm,
        scratch_shapes=[
            pltpu.VMEM((3, n_col, rows, width), BF16),
            pltpu.VMEM(part, BF16),
            pltpu.VMEM(part, BF16),
            pltpu.VMEM(part, BF16),
            pltpu.SemaphoreType.DMA,
            pltpu.SemaphoreType.DMA((n_row,)),
        ],
        compiler_params=pltpu.CompilerParams(vmem_limit_bytes=56 * 1024 * 1024),
        name="place",
    )(held)
    return coarse.reshape(n_col, n_row * n_col, rows, width)


def solution(mesh):
    return jax.shard_map(
        on_device,
        mesh=mesh,
        in_specs=(
            P(("row", "col"), None, None),
            P(("row", "col"), None),
            P(("row", "col"), None),
            P(),
            P(),
        ),
        out_specs=P("row", None, "col", None),
        check_vma=False,
    )
```

```python
import functools

import jax
import jax.numpy as jnp
from jax import lax
from jax.experimental import pallas as pl
from jax.experimental.pallas import tpu as pltpu
from jax.sharding import PartitionSpec as P

MESH = pl.DeviceIdType.MESH
F32 = jnp.float32
BF16 = jnp.bfloat16


def tdot(left, right):
    return lax.dot_general(left, right, (((0,), (0,)), ((), ())), preferred_element_type=F32)


def exchange_kernel(
    n_row, n_col, group,
    index, owner, margin, stiff_hbm, modes_hbm, out,
    stiff, modes, products, sums, applied, far_out, far_in, slots, held, total, before, last,
    stiff_sem, modes_sem, far_send, far_recv, piece_send, piece_recv,
):
    block_total, size, width = stiff.shape
    blocks = modes.shape[0]
    shared = far_out.shape[1]
    my_row = lax.axis_index("row")
    my_col = lax.axis_index("col")
    here = my_row * n_col + my_col
    back = lax.rem(my_row, 2)
    ends = (my_col - 1 + 2 * back, my_row - 1)
    starts = (my_col + 1 - 2 * back, my_row + 1)
    sends = (jnp.logical_and(ends[0] >= 0, ends[0] < n_col), ends[1] >= 0)
    takes = (jnp.logical_and(starts[0] >= 0, starts[0] < n_col), starts[1] < n_row)
    send_first = (here - 1 + back, here - n_col)
    take_first = (here - back, here)
    send_side = (1 - back, 1)
    take_side = (back, 0)
    target = ({"col": jnp.clip(ends[0], 0, n_col - 1)}, {"row": jnp.maximum(ends[1], 0)})
    next_row = {"row": jnp.minimum(starts[1], n_row - 1)}

    modes_copy = pltpu.make_async_copy(modes_hbm, modes, modes_sem)
    modes_copy.start()

    def stiff_copy(c):
        part = pl.ds(c * group, group)
        return pltpu.make_async_copy(stiff_hbm.at[part], stiff.at[part], stiff_sem.at[c])

    def start_stiff(c, carry):
        stiff_copy(c).start()
        return carry

    lax.fori_loop(0, block_total // group, start_stiff, 0)

    barrier = pltpu.get_barrier_semaphore()
    for d in range(1, n_col):
        pl.semaphore_signal(
            barrier, inc=1, device_id={"col": lax.rem(my_col + d, n_col)}, device_id_type=MESH
        )

    @pl.when(sends[1])
    def _():
        pl.semaphore_signal(barrier, inc=1, device_id=target[1], device_id_type=MESH)

    @pl.when(takes[1])
    def _():
        pl.semaphore_signal(barrier, inc=1, device_id=next_row, device_id_type=MESH)

    sums[0] = jnp.zeros((size, width), F32)
    latest = [jnp.int32(0)] * blocks
    for k in range(block_total):
        mine = index[0, k]
        found = jnp.int32(0)
        for a in range(blocks):
            hit = mine == a
            found = jnp.where(hit, latest[a], found)
            latest[a] = jnp.where(hit, k + 1, latest[a])
        before[k] = found
    for a in range(blocks):
        last[a] = latest[a]
    modes_copy.wait()

    slot_count = products.shape[0]

    def add_product(k):
        sums[k + 1] = sums[before[k]] + products[k % slot_count]

    for k in range(block_total):
        if k % group == 0:
            stiff_copy(k // group).wait()
        products[k % slot_count] = jnp.dot(
            stiff[k], modes[index[1, k]], preferred_element_type=F32
        )
        if k > 0:
            add_product(k - 1)
    add_product(block_total - 1)

    sides = sends[1].astype(jnp.int32) + takes[1].astype(jnp.int32)
    pl.semaphore_wait(barrier, n_col - 1 + sides)

    def far_copy(d, i):
        return pltpu.make_async_remote_copy(
            src_ref=far_out.at[d, i], dst_ref=far_in.at[d, i],
            send_sem=far_send.at[d, i], recv_sem=far_recv.at[d, i],
            device_id=target[d], device_id_type=MESH,
        )

    for d in range(2):
        @pl.when(sends[d])
        def _():
            first = send_first[d]
            flag = owner[d, first]
            for i in range(shared):
                pick = margin[d, i, send_side[d], first]
                far_out[d, i] = jnp.where(
                    flag + send_side[d] == 1, sums[last[pick]].astype(BF16), modes[pick]
                )
                far_copy(d, i).start()

    def piece_copy(slot, d):
        place = my_col - back if slot == 1 else my_col
        peer = lax.rem(my_col + d, n_col)
        return pltpu.make_async_remote_copy(
            src_ref=slots.at[slot, peer], dst_ref=held.at[slot, place],
            send_sem=piece_send.at[slot, d], recv_sem=piece_recv.at[slot, d],
            device_id={"col": peer}, device_id_type=MESH,
        )

    def scatter(slot, value):
        place = my_col - back if slot == 1 else my_col
        slots[slot] = value.astype(BF16).reshape(slots.shape[1:])
        for d in range(1, n_col):
            piece_copy(slot, d).start()
        held[slot, place] = slots[slot, my_col]

    def round_block(a, carry):
        applied[a] = sums[last[a]].astype(BF16)
        return carry

    lax.fori_loop(0, blocks, round_block, 0)
    step = 4 if blocks % 4 == 0 else 1
    total[...] = jnp.zeros_like(total)

    def diagonal_step(c, carry):
        part = pl.ds(c * step, step)
        total[...] += tdot(
            modes[part].reshape(step * size, width), applied[part].reshape(step * size, width)
        )
        return carry

    lax.fori_loop(0, blocks // step, diagonal_step, 0)
    scatter(0, total[...])

    for d in (1, 0):
        @pl.when(takes[d])
        def _():
            first = take_first[d]
            flag = owner[d, first]
            value = None
            for i in range(shared):
                pick = margin[d, i, take_side[d], first]
                near = jnp.where(flag + take_side[d] == 1, applied[pick], modes[pick])
                far_copy(d, i).wait_recv()
                far = far_in[d, i]
                if d == 0:
                    near, far = jnp.where(back == 0, near, far), jnp.where(back == 0, far, near)
                term = tdot(near, far)
                value = term if value is None else value + term
            scatter(d + 1, value)

    @pl.when(jnp.logical_not(takes[1]))
    def _():
        held[2] = jnp.zeros(held.shape[1:], BF16)

    held[1, n_col - 1] = jnp.zeros(held.shape[2:], BF16)

    for d in range(2):
        @pl.when(sends[d])
        def _():
            for i in range(shared):
                far_copy(d, i).wait_send()

    def wait_piece(slot, d):
        source = lax.rem(my_col + n_col - d, n_col)
        place = jnp.clip(source - back, 0, n_col - 1) if slot == 1 else source
        return pltpu.make_async_remote_copy(
            src_ref=slots.at[slot, my_col], dst_ref=held.at[slot, place],
            send_sem=piece_send.at[slot, d], recv_sem=piece_recv.at[slot, d],
            device_id={"col": lax.rem(my_col + d, n_col)}, device_id_type=MESH,
        )

    for d in range(1, n_col):
        wait_piece(0, d).wait_recv()
        piece_copy(0, d).wait_send()

    @pl.when(takes[1])
    def _():
        for d in range(1, n_col):
            wait_piece(2, d).wait_recv()
            piece_copy(2, d).wait_send()

    for d in range(1, n_col):
        origin = lax.rem(my_col + n_col - d, n_col) + 1 - 2 * back

        @pl.when(jnp.logical_and(origin >= 0, origin < n_col))
        def _():
            wait_piece(1, d).wait_recv()

        @pl.when(takes[0])
        def _():
            piece_copy(1, d).wait_send()

    out[...] = held[...]


def place_kernel(n_row, n_col, held_hbm, out, held, zeros, same, after, held_sem, out_sem):
    my_row = lax.axis_index("row")
    fetch = pltpu.make_async_copy(held_hbm, held, held_sem)
    fetch.start()
    zeros[...] = jnp.zeros_like(zeros)

    def write(source, g):
        return pltpu.make_async_copy(source, out.at[:, g], out_sem.at[g])

    for g in range(n_row):
        @pl.when(jnp.logical_and(g != my_row, g != my_row + 1))
        def _():
            write(zeros, g).start()

    same[...] = jnp.zeros_like(same)
    after[...] = jnp.zeros_like(after)
    fetch.wait()
    for i in range(n_col):
        same[i, i] = held[0, i]
        if i < n_col - 1:
            same[i, i + 1] = held[1, i]
    write(same, my_row).start()

    @pl.when(my_row < n_row - 1)
    def _():
        for i in range(n_col):
            after[i, i] = held[2, i]
        write(after, my_row + 1).start()

    for g in range(n_row):
        write(zeros, g).wait()


def on_device(stiffness, stiffness_index, mode_basis, pair_owner, margin):
    n_row = lax.axis_size("row")
    n_col = lax.axis_size("col")
    count, size, _ = stiffness.shape
    width = mode_basis.shape[1]
    blocks = mode_basis.shape[0] // size
    shared = margin.shape[2]
    rows = width // n_col
    group = max(q for q in range(1, 9) if count % q == 0)
    smem = pl.BlockSpec(memory_space=pltpu.SMEM)
    hbm = pl.BlockSpec(memory_space=pl.ANY)
    held = pl.pallas_call(
        functools.partial(exchange_kernel, n_row, n_col, group),
        out_shape=jax.ShapeDtypeStruct((3, n_col, rows, width), BF16),
        in_specs=[smem] * 3 + [hbm] * 2,
        out_specs=pl.BlockSpec(memory_space=pltpu.VMEM),
        scratch_shapes=[
            pltpu.VMEM((count, size, size), BF16),
            pltpu.VMEM((blocks, size, width), BF16),
            pltpu.VMEM((4, size, width), F32),
            pltpu.VMEM((count + 1, size, width), F32),
            pltpu.VMEM((blocks, size, width), BF16),
            pltpu.VMEM((2, shared, size, width), BF16),
            pltpu.VMEM((2, shared, size, width), BF16),
            pltpu.VMEM((3, n_col, rows, width), BF16),
            pltpu.VMEM((3, n_col, rows, width), BF16),
            pltpu.VMEM((width, width), F32),
            pltpu.SMEM((count,), jnp.int32),
            pltpu.SMEM((blocks,), jnp.int32),
            pltpu.SemaphoreType.DMA((count // group,)),
            pltpu.SemaphoreType.DMA,
            pltpu.SemaphoreType.DMA((2, shared)),
            pltpu.SemaphoreType.DMA((2, shared)),
            pltpu.SemaphoreType.DMA((3, n_col)),
            pltpu.SemaphoreType.DMA((3, n_col)),
        ],
        compiler_params=pltpu.CompilerParams(
            collective_id=0, has_side_effects=True, vmem_limit_bytes=56 * 1024 * 1024
        ),
        name="exchange",
    )(
        stiffness_index.T,
        pair_owner.T,
        margin.transpose(1, 2, 3, 0),
        stiffness,
        mode_basis.reshape(blocks, size, width),
    )
    part = (n_col, n_col, rows, width)
    coarse = pl.pallas_call(
        functools.partial(place_kernel, n_row, n_col),
        out_shape=jax.ShapeDtypeStruct((n_col, n_row, n_col, rows, width), BF16),
        in_specs=[hbm],
        out_specs=hbm,
        scratch_shapes=[
            pltpu.VMEM((3, n_col, rows, width), BF16),
            pltpu.VMEM(part, BF16),
            pltpu.VMEM(part, BF16),
            pltpu.VMEM(part, BF16),
            pltpu.SemaphoreType.DMA,
            pltpu.SemaphoreType.DMA((n_row,)),
        ],
        compiler_params=pltpu.CompilerParams(vmem_limit_bytes=56 * 1024 * 1024),
        name="place",
    )(held)
    return coarse.reshape(n_col, n_row * n_col, rows, width)


def solution(mesh):
    return jax.shard_map(
        on_device,
        mesh=mesh,
        in_specs=(
            P(("row", "col"), None, None),
            P(("row", "col"), None),
            P(("row", "col"), None),
            P(),
            P(),
        ),
        out_specs=P("row", None, "col", None),
        check_vma=False,
    )
```

```python
import functools

import jax
import jax.numpy as jnp
from jax import lax
from jax.experimental import pallas as pl
from jax.experimental.pallas import tpu as pltpu
from jax.sharding import PartitionSpec as P

MESH = pl.DeviceIdType.MESH
F32 = jnp.float32
BF16 = jnp.bfloat16


def tdot(left, right):
    return lax.dot_general(left, right, (((0,), (0,)), ((), ())), preferred_element_type=F32)


def exchange_kernel(
    n_row, n_col, group, passes,
    index, owner, margin, stiff_hbm, modes_hbm, out,
    stiff, modes, products, sums, applied, far_out, far_in, slots, held, total, before, last,
    stiff_sem, modes_sem, far_send, far_recv, piece_send, piece_recv,
):
    block_total, size, width = stiff.shape
    blocks = modes.shape[0]
    shared = far_out.shape[1] // passes
    half = size // passes
    my_row = lax.axis_index("row")
    my_col = lax.axis_index("col")
    here = my_row * n_col + my_col
    back = lax.rem(my_row, 2)
    ends = (my_col - 1 + 2 * back, my_row - 1)
    starts = (my_col + 1 - 2 * back, my_row + 1)
    sends = (jnp.logical_and(ends[0] >= 0, ends[0] < n_col), ends[1] >= 0)
    takes = (jnp.logical_and(starts[0] >= 0, starts[0] < n_col), starts[1] < n_row)
    send_first = (here - 1 + back, here - n_col)
    take_first = (here - back, here)
    send_side = (1 - back, 1)
    take_side = (back, 0)
    target = ({"col": jnp.clip(ends[0], 0, n_col - 1)}, {"row": jnp.maximum(ends[1], 0)})
    next_row = {"row": jnp.minimum(starts[1], n_row - 1)}

    modes_copy = pltpu.make_async_copy(modes_hbm, modes, modes_sem)
    modes_copy.start()

    chunks = block_total // group

    def stiff_copy(h, c):
        part = (pl.ds(c * group, group), pl.ds(h * half, half))
        return pltpu.make_async_copy(stiff_hbm.at[part], stiff.at[part], stiff_sem.at[h, c])

    for h in range(passes):
        for c in range(chunks):
            stiff_copy(h, c).start()

    barrier = pltpu.get_barrier_semaphore()
    for d in range(1, n_col):
        pl.semaphore_signal(
            barrier, inc=1, device_id={"col": lax.rem(my_col + d, n_col)}, device_id_type=MESH
        )

    @pl.when(sends[1])
    def _():
        pl.semaphore_signal(barrier, inc=1, device_id=target[1], device_id_type=MESH)

    @pl.when(takes[1])
    def _():
        pl.semaphore_signal(barrier, inc=1, device_id=next_row, device_id_type=MESH)

    sums[0] = jnp.zeros((size, width), F32)
    latest = [jnp.int32(0)] * blocks
    for k in range(block_total):
        mine = index[0, k]
        found = jnp.int32(0)
        for a in range(blocks):
            hit = mine == a
            found = jnp.where(hit, latest[a], found)
            latest[a] = jnp.where(hit, k + 1, latest[a])
        before[k] = found
    for a in range(blocks):
        last[a] = latest[a]
    modes_copy.wait()

    def far_copy(d, j):
        return pltpu.make_async_remote_copy(
            src_ref=far_out.at[d, j], dst_ref=far_in.at[d, j],
            send_sem=far_send.at[d, j], recv_sem=far_recv.at[d, j],
            device_id=target[d], device_id_type=MESH,
        )

    sides = sends[1].astype(jnp.int32) + takes[1].astype(jnp.int32)
    for h in range(passes):
        rows = pl.ds(h * half, half)

        def apply_group(c, carry):
            stiff_copy(h, c).wait()
            for q in range(group):
                k = c * group + q
                products[q] = jnp.dot(
                    stiff[k, rows], modes[index[1, k]], preferred_element_type=F32
                )
            for q in range(group):
                k = c * group + q
                sums[k + 1, rows] = sums[before[k], rows] + products[q]
            return carry

        lax.fori_loop(0, chunks, apply_group, 0)
        if h == 0:
            pl.semaphore_wait(barrier, n_col - 1 + sides)
        for d in range(2):
            @pl.when(sends[d])
            def _():
                first = send_first[d]
                flag = owner[d, first]
                for i in range(shared):
                    pick = margin[d, i, send_side[d], first]
                    j = h * shared + i
                    far_out[d, j] = jnp.where(
                        flag + send_side[d] == 1,
                        sums[last[pick], rows].astype(BF16),
                        modes[pick, rows],
                    )
                    far_copy(d, j).start()

    def piece_copy(slot, d):
        place = my_col - back if slot == 1 else my_col
        peer = lax.rem(my_col + d, n_col)
        return pltpu.make_async_remote_copy(
            src_ref=slots.at[slot, peer], dst_ref=held.at[slot, place],
            send_sem=piece_send.at[slot, d], recv_sem=piece_recv.at[slot, d],
            device_id={"col": peer}, device_id_type=MESH,
        )

    def scatter(slot, value):
        place = my_col - back if slot == 1 else my_col
        slots[slot] = value.astype(BF16).reshape(slots.shape[1:])
        for d in range(1, n_col):
            piece_copy(slot, d).start()
        held[slot, place] = slots[slot, my_col]

    def round_block(a, carry):
        applied[a] = sums[last[a]].astype(BF16)
        return carry

    lax.fori_loop(0, blocks, round_block, 0)
    step = 4 if blocks % 4 == 0 else 1
    total[...] = jnp.zeros_like(total)

    def diagonal_step(c, carry):
        part = pl.ds(c * step, step)
        total[...] += tdot(
            modes[part].reshape(step * size, width), applied[part].reshape(step * size, width)
        )
        return carry

    lax.fori_loop(0, blocks // step, diagonal_step, 0)
    scatter(0, total[...])

    for d in (1, 0):
        @pl.when(takes[d])
        def _():
            first = take_first[d]
            flag = owner[d, first]
            value = None
            for j in range(passes * shared):
                h, i = divmod(j, shared)
                rows = pl.ds(h * half, half)
                pick = margin[d, i, take_side[d], first]
                near = jnp.where(
                    flag + take_side[d] == 1, applied[pick, rows], modes[pick, rows]
                )
                far_copy(d, j).wait_recv()
                far = far_in[d, j]
                if d == 0:
                    near, far = jnp.where(back == 0, near, far), jnp.where(back == 0, far, near)
                term = tdot(near, far)
                value = term if value is None else value + term
            scatter(d + 1, value)

    @pl.when(jnp.logical_not(takes[1]))
    def _():
        held[2] = jnp.zeros(held.shape[1:], BF16)

    held[1, n_col - 1] = jnp.zeros(held.shape[2:], BF16)

    for d in range(2):
        @pl.when(sends[d])
        def _():
            for j in range(passes * shared):
                far_copy(d, j).wait_send()

    def wait_piece(slot, d):
        source = lax.rem(my_col + n_col - d, n_col)
        place = jnp.clip(source - back, 0, n_col - 1) if slot == 1 else source
        return pltpu.make_async_remote_copy(
            src_ref=slots.at[slot, my_col], dst_ref=held.at[slot, place],
            send_sem=piece_send.at[slot, d], recv_sem=piece_recv.at[slot, d],
            device_id={"col": lax.rem(my_col + d, n_col)}, device_id_type=MESH,
        )

    for d in range(1, n_col):
        wait_piece(0, d).wait_recv()
        piece_copy(0, d).wait_send()

    @pl.when(takes[1])
    def _():
        for d in range(1, n_col):
            wait_piece(2, d).wait_recv()
            piece_copy(2, d).wait_send()

    for d in range(1, n_col):
        origin = lax.rem(my_col + n_col - d, n_col) + 1 - 2 * back

        @pl.when(jnp.logical_and(origin >= 0, origin < n_col))
        def _():
            wait_piece(1, d).wait_recv()

        @pl.when(takes[0])
        def _():
            piece_copy(1, d).wait_send()

    out[...] = held[...]


def place_kernel(n_row, n_col, held_hbm, out, held, zeros, same, after, held_sem, out_sem):
    my_row = lax.axis_index("row")
    fetch = pltpu.make_async_copy(held_hbm, held, held_sem)
    fetch.start()
    zeros[...] = jnp.zeros_like(zeros)

    def write(source, g):
        return pltpu.make_async_copy(source, out.at[:, g], out_sem.at[g])

    for g in range(n_row):
        @pl.when(jnp.logical_and(g != my_row, g != my_row + 1))
        def _():
            write(zeros, g).start()

    same[...] = jnp.zeros_like(same)
    after[...] = jnp.zeros_like(after)
    fetch.wait()
    for i in range(n_col):
        same[i, i] = held[0, i]
        if i < n_col - 1:
            same[i, i + 1] = held[1, i]
    write(same, my_row).start()

    @pl.when(my_row < n_row - 1)
    def _():
        for i in range(n_col):
            after[i, i] = held[2, i]
        write(after, my_row + 1).start()

    for g in range(n_row):
        write(zeros, g).wait()


def on_device(stiffness, stiffness_index, mode_basis, pair_owner, margin):
    n_row = lax.axis_size("row")
    n_col = lax.axis_size("col")
    count, size, _ = stiffness.shape
    width = mode_basis.shape[1]
    blocks = mode_basis.shape[0] // size
    shared = margin.shape[2]
    rows = width // n_col
    group = max(q for q in range(1, 9) if count % q == 0)
    smem = pl.BlockSpec(memory_space=pltpu.SMEM)
    hbm = pl.BlockSpec(memory_space=pl.ANY)
    passes = 2
    held = pl.pallas_call(
        functools.partial(exchange_kernel, n_row, n_col, group, passes),
        out_shape=jax.ShapeDtypeStruct((3, n_col, rows, width), BF16),
        in_specs=[smem] * 3 + [hbm] * 2,
        out_specs=pl.BlockSpec(memory_space=pltpu.VMEM),
        scratch_shapes=[
            pltpu.VMEM((count, size, size), BF16),
            pltpu.VMEM((blocks, size, width), BF16),
            pltpu.VMEM((group, size // passes, width), F32),
            pltpu.VMEM((count + 1, size, width), F32),
            pltpu.VMEM((blocks, size, width), BF16),
            pltpu.VMEM((2, passes * shared, size // passes, width), BF16),
            pltpu.VMEM((2, passes * shared, size // passes, width), BF16),
            pltpu.VMEM((3, n_col, rows, width), BF16),
            pltpu.VMEM((3, n_col, rows, width), BF16),
            pltpu.VMEM((width, width), F32),
            pltpu.SMEM((count,), jnp.int32),
            pltpu.SMEM((blocks,), jnp.int32),
            pltpu.SemaphoreType.DMA((passes, count // group)),
            pltpu.SemaphoreType.DMA,
            pltpu.SemaphoreType.DMA((2, passes * shared)),
            pltpu.SemaphoreType.DMA((2, passes * shared)),
            pltpu.SemaphoreType.DMA((3, n_col)),
            pltpu.SemaphoreType.DMA((3, n_col)),
        ],
        compiler_params=pltpu.CompilerParams(
            collective_id=0, has_side_effects=True, vmem_limit_bytes=56 * 1024 * 1024
        ),
        name="exchange",
    )(
        stiffness_index.T,
        pair_owner.T,
        margin.transpose(1, 2, 3, 0),
        stiffness,
        mode_basis.reshape(blocks, size, width),
    )
    part = (n_col, n_col, rows, width)
    coarse = pl.pallas_call(
        functools.partial(place_kernel, n_row, n_col),
        out_shape=jax.ShapeDtypeStruct((n_col, n_row, n_col, rows, width), BF16),
        in_specs=[hbm],
        out_specs=hbm,
        scratch_shapes=[
            pltpu.VMEM((3, n_col, rows, width), BF16),
            pltpu.VMEM(part, BF16),
            pltpu.VMEM(part, BF16),
            pltpu.VMEM(part, BF16),
            pltpu.SemaphoreType.DMA,
            pltpu.SemaphoreType.DMA((n_row,)),
        ],
        compiler_params=pltpu.CompilerParams(vmem_limit_bytes=56 * 1024 * 1024),
        name="place",
    )(held)
    return coarse.reshape(n_col, n_row * n_col, rows, width)


def solution(mesh):
    return jax.shard_map(
        on_device,
        mesh=mesh,
        in_specs=(
            P(("row", "col"), None, None),
            P(("row", "col"), None),
            P(("row", "col"), None),
            P(),
            P(),
        ),
        out_specs=P("row", None, "col", None),
        check_vma=False,
    )
```
